256 devices in a mesh: grp: 16 (over x_hi, z), blk: 16 (over y, x_lo, core).
Axes of the slice: x: 4 (x_hi: 2, x_lo: 2; x = x_hi * 2 + x_lo), y: 4, z: 8, core: 2. Of those that a mesh axis runs over, the one named last changes fastest.
Arguments:
- queries: bfloat16 [32768, 2048], P(('grp', 'blk')), parts along dimension 0, may hold values from -8 to 8
- keys: bfloat16 [32768, 1024], P(('grp', 'blk')), parts along dimension 0, may hold values from -8 to 8
- values: bfloat16 [32768, 1024], P(('grp', 'blk')), parts along dimension 0, may hold values from -6 to 6
- dout: bfloat16 [32768, 2048], P(('grp', 'blk')), parts along dimension 0, may hold values from -6 to 6
- segments: int32 [32768], P(('grp', 'blk')), parts along dimension 0, may hold values from 0 to 7, never falling along the last dimension, each value on 1 to 1024 neighbouring positions
Outputs:
- grad_queries: bfloat16 [32768, 2048], P(('grp', 'blk')), parts along dimension 0
- keys_gradient: bfloat16 [32768, 1024], P(('grp', 'blk')), parts along dimension 0
- values_gradient: bfloat16 [32768, 1024], P(('grp', 'blk')), parts along dimension 0
The draws below stay inside these ranges and needn't reach their ends.
There are 16 independent parts, one for each index of `grp`. The reference program is written for one: setup_inputs(seed, part) draws one part's arguments, and reference() takes and returns one part's arrays. A program takes and returns all parts, laid end to end along the dimension named above; each array names one. Nothing has to cross between parts.
Inputs may be any that keep to these rules, and one draw needn't show every extreme that they name: segments never fall along the sequence; each of the 8 documents has 1 to 1024 tokens and one has exactly 1024.
All inputs are finite; a program needn't handle non-finite values.
Results may differ from the reference program's by a relative error of at most 0.015.
Values may be sent and summed in bfloat16 or wider, within the bound.
No kernel may reach another device: no remote copies, remote signals or barrier semaphores. Data moves between devices by JAX's collectives and lax.ppermute only.
A program may use at most 128 MiB of HBM per device.

```python
import math
import jax
import jax.numpy as jnp
import numpy as np
from jax import lax

HQ = 16
KV_HEAD_COUNT = 8
HEAD_SIZE = 128
QUERY_PER_KV = 2
DOCS = 8
PACKED_TOKENS = 2048


def shared_direction(key):
    return jax.random.rademacher(key, (KV_HEAD_COUNT, HEAD_SIZE), dtype=jnp.float32)


def build_rows(key, direction, array_shape, low_level, high_level):
    noise_key, level_key, chosen_key = jax.random.split(key, 3)
    noise = jax.random.normal(noise_key, array_shape, jnp.float32)
    level_shape = (array_shape[0], array_shape[1]) + (1,) * (len(array_shape) - 2)
    level = jax.random.uniform(level_key, level_shape, jnp.float32, low_level, high_level)
    chosen = (jax.random.uniform(chosen_key, (array_shape[0],) + (1,) * (len(array_shape) - 1), jnp.float32) < 0.125).astype(jnp.float32)
    return chosen * level * direction + (1.0 - 0.5 * chosen) * noise


def draw_queries(key, part):
    direction = shared_direction(key)
    key = jax.random.fold_in(key, 11)
    array_shape = (PACKED_TOKENS, KV_HEAD_COUNT, QUERY_PER_KV, HEAD_SIZE)
    aligned = direction[None, :, None, :]
    row_range = build_rows(key, aligned, array_shape, 1.5, 3.0)
    row_range = jnp.clip(row_range, -8.0, 8.0)
    return row_range.reshape(PACKED_TOKENS, HQ * HEAD_SIZE).astype(jnp.bfloat16)


def draw_keys(key, part):
    direction = shared_direction(key)
    key = jax.random.fold_in(key, 12)
    array_shape = (PACKED_TOKENS, KV_HEAD_COUNT, HEAD_SIZE)
    aligned = direction[None, :, :]
    row_range = build_rows(key, aligned, array_shape, 1.5, 3.0)
    row_range = jnp.clip(row_range, -8.0, 8.0)
    return row_range.reshape(PACKED_TOKENS, KV_HEAD_COUNT * HEAD_SIZE).astype(jnp.bfloat16)


def block_levels(key, extent, cuts, least, top_value):
    factor_of, own = 1.0, jax.random.fold_in(key, 6)
    for axis_at, blocks in cuts:
        steps = jnp.exp(jax.random.uniform(jax.random.fold_in(own, axis_at), (blocks,), jnp.float32, least / len(cuts), top_value / len(cuts)))
        factor_of = factor_of * jnp.repeat(steps, extent[axis_at] // blocks).reshape([-1 if axis == axis_at else 1 for axis in range(len(extent))])
    return factor_of


def profile(number_of, total, limit, skew):
    loads = [(1 << 20) // math.isqrt(grade ** skew) + 1 for grade in range(2, number_of + 1)]
    surplus, holding = total - limit - (number_of - 1), [1] * (number_of - 1)
    while surplus > 0:
        candidates = [i for i in range(number_of - 1) if holding[i] < limit]
        mass, left = sum([loads[i] for i in candidates]), surplus
        for i in candidates:
            addition = min(limit - holding[i], max(1, left * loads[i] // mass), surplus)
            holding[i] = holding[i] + addition
            surplus = surplus - addition
    return np.array([limit] + holding)


def uneven_parts(own_key, number_of, total, most, slope):
    if number_of == 2:
        one = jax.random.randint(own_key, (), max(1, total - most), min(most, total - 1) + 1)
        return jnp.stack([one, total - one])
    tallies = jnp.asarray(profile(number_of, total, most, slope), jnp.int32)
    couples = (number_of - 1) // 2
    giver, sink = tallies[1:1 + 2 * couples:2], tallies[2:2 + 2 * couples:2]
    margin = jnp.minimum(giver - 1, most - sink)
    moved = jax.random.randint(jax.random.fold_in(own_key, 1), (couples,), 0, 1 << 20) % (margin + 1)
    tallies = tallies.at[1:1 + 2 * couples:2].set(giver - moved).at[2:2 + 2 * couples:2].set(sink + moved)
    return tallies[jax.random.permutation(jax.random.fold_in(own_key, 2), number_of)]


def scatter_about(rng, dims, scale, limit, shards=(), held_as=jnp.bfloat16):
    level = block_levels(rng, dims, shards, -0.22, 0.18) if shards else 1.0
    array = jax.random.normal(rng, dims, jnp.float32) * scale * level
    return jnp.minimum(jnp.maximum(array, -limit), limit).astype(held_as)


def setup_inputs(seed: int = 0, part: int = 0) -> dict:
    streams_of = jax.random.split(jax.random.key(seed), 6)
    part_splits = jax.random.split(jax.random.fold_in(streams_of[5], part), 6)
    queries = draw_queries(jax.random.fold_in(jax.random.fold_in(streams_of[5], part), 71), part)
    keys = draw_keys(jax.random.fold_in(jax.random.fold_in(streams_of[5], part), 71), part)
    values = scatter_about(part_splits[2], (PACKED_TOKENS, KV_HEAD_COUNT * HEAD_SIZE), 1.0, 6.0, ((0, 16),))
    dout = scatter_about(part_splits[3], (PACKED_TOKENS, HQ * HEAD_SIZE), 1.0, 6.0, ((0, 16),))
    segments = jnp.searchsorted(jnp.cumsum(uneven_parts(part_splits[4], DOCS, PACKED_TOKENS, PACKED_TOKENS // 2, 2)), jnp.arange(PACKED_TOKENS), side="right").astype(jnp.int32)
    return {"queries": queries, "keys": keys, "values": values, "dout": dout, "segments": segments}


score_scale = 1.0 / 12.0
cap_value = 50.0


def reference(queries, keys, values, dout, segments):
    token_length = queries.shape[0]
    position = jnp.arange(token_length, dtype=jnp.int32)
    visible = (position[None, :] <= position[:, None]) & (segments[None, :] == segments[:, None])
    heads_of_queries = queries.reshape(token_length, KV_HEAD_COUNT, QUERY_PER_KV, HEAD_SIZE).transpose(1, 2, 0, 3)
    output_grad_heads = dout.reshape(token_length, KV_HEAD_COUNT, QUERY_PER_KV, HEAD_SIZE).transpose(1, 2, 0, 3)
    heads_of_keys = keys.reshape(token_length, KV_HEAD_COUNT, HEAD_SIZE).transpose(1, 0, 2)
    heads_of_values = values.reshape(token_length, KV_HEAD_COUNT, HEAD_SIZE).transpose(1, 0, 2)

    def one_group(operands):
        query_part, dout_part, key_part, value_part = operands
        query_wide = query_part.astype(jnp.float32)
        dout_wide = dout_part.astype(jnp.float32)
        key_wide = key_part.astype(jnp.float32)
        value_wide = value_part.astype(jnp.float32)
        raw = jnp.einsum("rid,jd->rij", query_wide, key_wide)
        capped = jnp.tanh(raw * score_scale / cap_value)
        expo = jnp.where(visible[None], jnp.exp(cap_value * capped), jnp.float32(0.0))
        total = jnp.sum(expo, axis=-1)
        dprob = jnp.einsum("rid,jd->rij", dout_wide, value_wide)
        delta = jnp.sum(expo * dprob, axis=-1) / total
        prob = expo / total[..., None]
        prob_low = prob.astype(jnp.bfloat16)
        dscore = prob * (dprob - delta[..., None]) * (1.0 - capped * capped) * score_scale
        dscore_low = dscore.astype(jnp.bfloat16)
        grad_query = jnp.einsum("rij,jd->rid", dscore_low.astype(jnp.float32), key_wide)
        grad_key = jnp.einsum("rij,rid->jd", dscore_low.astype(jnp.float32), query_wide)
        grad_value = jnp.einsum("rij,rid->jd", prob_low.astype(jnp.float32), dout_wide)
        return (grad_query.astype(jnp.bfloat16), grad_key.astype(jnp.bfloat16), grad_value.astype(jnp.bfloat16))

    grad_q, key_gradient_part, value_gradient_part = lax.map(one_group, (heads_of_queries, output_grad_heads, heads_of_keys, heads_of_values))
    grad_queries = grad_q.transpose(2, 0, 1, 3).reshape(token_length, HQ * HEAD_SIZE)
    keys_gradient = key_gradient_part.transpose(1, 0, 2).reshape(token_length, KV_HEAD_COUNT * HEAD_SIZE)
    values_gradient = value_gradient_part.transpose(1, 0, 2).reshape(token_length, KV_HEAD_COUNT * HEAD_SIZE)
    return (grad_queries, keys_gradient, values_gradient)
```

```python
import math
import jax
import jax.numpy as jnp
from jax import lax
from jax.experimental import pallas as pl
from jax.experimental.pallas import tpu as pltpu
from jax.sharding import PartitionSpec as P

HQ = 16
KV_HEAD_COUNT = 8
HEAD_SIZE = 128
DOCS = 8
BLOCKS = 16
ROWS = 128
SEG_ROWS = 16
IN_ROWS = 3 * ROWS + SEG_ROWS
TILE = 256
TILES = BLOCKS * ROWS // TILE
WIDEST = 5

score_scale = 1.0 / 12.0
cap_value = 50.0
to_cap = score_scale / cap_value
cap_log2 = cap_value * math.log2(math.e)

NT = (((1,), (1,)), ((), ()))
VMEM_LIMIT = 48 * 1024 * 1024


def vmem():
    return pl.BlockSpec(memory_space=pltpu.VMEM)


def pack_kernel(q_ref, k_ref, v_ref, do_ref, seg_ref, out_ref):
    seg = jnp.broadcast_to(seg_ref[...].astype(jnp.float32), (SEG_ROWS, ROWS)).astype(jnp.bfloat16)
    for h in range(HQ):
        kv_ref = k_ref if h % 2 == 0 else v_ref
        g = h // 2
        out_ref[h, 0:ROWS, :] = q_ref[:, h * HEAD_SIZE : (h + 1) * HEAD_SIZE]
        out_ref[h, ROWS : 2 * ROWS, :] = do_ref[:, h * HEAD_SIZE : (h + 1) * HEAD_SIZE]
        out_ref[h, 2 * ROWS : 3 * ROWS, :] = kv_ref[:, g * HEAD_SIZE : (g + 1) * HEAD_SIZE]
        out_ref[h, 3 * ROWS :, :] = seg


def unpack_kernel(in_ref, dq_ref, dk_ref, dv_ref):
    for h in range(HQ):
        out_ref = dk_ref if h % 2 == 0 else dv_ref
        g = h // 2
        dq_ref[:, h * HEAD_SIZE : (h + 1) * HEAD_SIZE] = in_ref[h, 0:ROWS, :]
        out_ref[:, g * HEAD_SIZE : (g + 1) * HEAD_SIZE] = in_ref[h, ROWS : 2 * ROWS, :]


def main_kernel(
    core_ref, in_ref, other_ref, dq_ref, keep_ref, send_ref,
    k_s, v_s, kt_s, first_s, low_s, dk_s, dv_s,
):
    is_k = core_ref[0] == 0
    for b in range(BLOCKS):
        mine = in_ref[b, 2 * ROWS : 3 * ROWS, :]
        theirs = other_ref[b]
        key = jnp.where(is_k, mine, theirs)
        k_s[b * ROWS : (b + 1) * ROWS, :] = key
        v_s[b * ROWS : (b + 1) * ROWS, :] = jnp.where(is_k, theirs, mine)
        kt_s[:, b * ROWS : (b + 1) * ROWS] = key.T
    dk_s[...] = jnp.zeros_like(dk_s)
    dv_s[...] = jnp.zeros_like(dv_s)

    seg = jnp.concatenate(
        [in_ref[b, 3 * ROWS : IN_ROWS, :][:1].astype(jnp.float32) for b in range(BLOCKS)], axis=0
    )
    first = jnp.zeros_like(seg)
    for d in range(1, DOCS):
        below = jnp.where(seg < float(d), 1.0, 0.0)
        start = jnp.sum(jnp.sum(below, axis=1, keepdims=True), axis=0, keepdims=True)
        first = jnp.where(seg == float(d), start, first)
    first = first.astype(jnp.int32)
    first_s[...] = first
    for i in range(TILES):
        low_s[i] = jnp.min(first[2 * i : 2 * i + 1, :]) // TILE

    def one_block(i, low, width):
        keys = width * TILE
        base = pl.multiple_of(low * TILE, TILE)
        q = in_ref[pl.ds(2 * i, 2), 0:ROWS, :].reshape(TILE, HEAD_SIZE)
        do = in_ref[pl.ds(2 * i, 2), ROWS : 2 * ROWS, :].reshape(TILE, HEAD_SIZE)
        start = jnp.concatenate([first_s[pl.ds(2 * i, 1), :], first_s[pl.ds(2 * i + 1, 1), :]], axis=1)
        key_pos = base + lax.broadcasted_iota(jnp.int32, (keys, TILE), 0)
        query_pos = i * TILE + lax.broadcasted_iota(jnp.int32, (1, TILE), 1)
        visible = (key_pos >= start) & (key_pos <= query_pos)
        raw = lax.dot_general(k_s[pl.ds(base, keys), :], q, NT, preferred_element_type=jnp.float32)
        dprob = lax.dot_general(v_s[pl.ds(base, keys), :], do, NT, preferred_element_type=jnp.float32)
        capped = jnp.tanh(raw * to_cap)
        expo = jnp.where(visible, jnp.exp2(capped * cap_log2), 0.0)
        total = jnp.sum(expo, axis=0, keepdims=True)
        inverse = 1.0 / total
        delta = jnp.sum(expo * dprob, axis=0, keepdims=True) * inverse
        prob = expo * inverse
        dscore = prob * (dprob - delta) * (1.0 - capped * capped)
        prob = prob.astype(jnp.bfloat16)
        dscore = dscore.astype(jnp.bfloat16)
        dv_s[pl.ds(base, keys), :] += jnp.dot(prob, do, preferred_element_type=jnp.float32)
        dk_s[pl.ds(base, keys), :] += jnp.dot(dscore, q, preferred_element_type=jnp.float32)
        dq = jnp.dot(kt_s[:, pl.ds(base, keys)], dscore, preferred_element_type=jnp.float32)
        dq = (dq * score_scale).T.astype(jnp.bfloat16)
        dq_ref[pl.ds(2 * i, 2)] = dq.reshape(2, ROWS, HEAD_SIZE)

    @pl.loop(0, TILES)
    def _(i):
        low = low_s[i]
        for width in range(1, WIDEST + 1):

            @pl.when(i - low + 1 == width)
            def _():
                one_block(i, low, width)

    for b in range(BLOCKS):
        dk = (dk_s[b * ROWS : (b + 1) * ROWS, :] * score_scale).astype(jnp.bfloat16)
        dv = dv_s[b * ROWS : (b + 1) * ROWS, :].astype(jnp.bfloat16)
        keep_ref[b] = jnp.where(is_k, dk, dv)
        send_ref[b] = jnp.where(is_k, dv, dk)


def join_kernel(dq_ref, keep_ref, got_ref, out_ref):
    out_ref[:, 0:ROWS, :] = dq_ref[...]
    total = keep_ref[...].astype(jnp.float32) + got_ref[...].astype(jnp.float32)
    out_ref[:, ROWS:, :] = total.astype(jnp.bfloat16)


def call(kernel, out_shape, operands, scratch=(), smem=0):
    return pl.pallas_call(
        kernel,
        out_shape=out_shape,
        in_specs=[pl.BlockSpec(memory_space=pltpu.SMEM)] * smem + [vmem()] * (len(operands) - smem),
        out_specs=jax.tree.map(lambda _: vmem(), out_shape),
        scratch_shapes=list(scratch),
        compiler_params=pltpu.CompilerParams(vmem_limit_bytes=VMEM_LIMIT),
    )(*operands)


def bf16(*shape):
    return jax.ShapeDtypeStruct(shape, jnp.bfloat16)


def body(queries, keys, values, dout, segments):
    swap = [(i, i ^ 1) for i in range(BLOCKS)]
    core = (lax.axis_index("blk") % 2).astype(jnp.int32).reshape(1)
    packed = call(
        pack_kernel,
        bf16(BLOCKS, IN_ROWS, HEAD_SIZE),
        (queries, keys, values, dout, segments.reshape(1, ROWS)),
    )
    mine = lax.all_to_all(packed, "blk", 0, 0, tiled=True)
    other = lax.ppermute(mine[:, 2 * ROWS : 3 * ROWS, :], "blk", swap)
    tokens = BLOCKS * ROWS
    dq, keep, send = call(
        main_kernel,
        (bf16(BLOCKS, ROWS, HEAD_SIZE),) * 3,
        (core, mine, other),
        scratch=(
            pltpu.VMEM((tokens, HEAD_SIZE), jnp.bfloat16),
            pltpu.VMEM((tokens, HEAD_SIZE), jnp.bfloat16),
            pltpu.VMEM((HEAD_SIZE, tokens), jnp.bfloat16),
            pltpu.VMEM((BLOCKS, ROWS), jnp.int32),
            pltpu.SMEM((TILES,), jnp.int32),
            pltpu.VMEM((tokens, HEAD_SIZE), jnp.float32),
            pltpu.VMEM((tokens, HEAD_SIZE), jnp.float32),
        ),
        smem=1,
    )
    got = lax.ppermute(send, "blk", swap)
    joined = call(join_kernel, bf16(BLOCKS, 2 * ROWS, HEAD_SIZE), (dq, keep, got))
    back = lax.all_to_all(joined, "blk", 0, 0, tiled=True)
    return call(
        unpack_kernel,
        (bf16(ROWS, HQ * HEAD_SIZE), bf16(ROWS, KV_HEAD_COUNT * HEAD_SIZE), bf16(ROWS, KV_HEAD_COUNT * HEAD_SIZE)),
        (back,),
    )


def solution(mesh):
    rows = P(("grp", "blk"), None)
    in_specs = (rows, rows, rows, rows, P(("grp", "blk")))
    return jax.shard_map(body, mesh=mesh, in_specs=in_specs, out_specs=(rows, rows, rows), check_vma=False)
```

```python
import math
import jax
import jax.numpy as jnp
from jax import lax
from jax.experimental import pallas as pl
from jax.experimental.pallas import tpu as pltpu
from jax.sharding import PartitionSpec as P

HEAD_SIZE = 128
DOCS = 8
CHIPS = 8
CORES = 2
ROWS = 128
PAIR = CORES * ROWS
SEG_ROWS = 16
DO_AT = PAIR
KV_AT = 2 * PAIR
KV_ROWS = 2 * ROWS + SEG_ROWS
IN_ROWS = KV_AT + KV_ROWS
TOKENS = CHIPS * PAIR
WIDEST = 9

score_scale = 1.0 / 12.0
cap_value = 50.0
to_cap = score_scale / cap_value
cap_log2 = cap_value * math.log2(math.e)

NT = (((1,), (1,)), ((), ()))
VMEM_LIMIT = 32 * 1024 * 1024

ANY = pl.BlockSpec(memory_space=pl.ANY)
HBM = pl.BlockSpec(memory_space=pltpu.HBM)
VMEM = pl.BlockSpec(memory_space=pltpu.VMEM)
SMEM = pl.BlockSpec(memory_space=pltpu.SMEM)


def bf16(*shape):
    return jax.ShapeDtypeStruct(shape, jnp.bfloat16)


def columns(h):
    return pl.ds(h * HEAD_SIZE, HEAD_SIZE)


def run_copies(pairs, sem):
    started = [pltpu.make_async_copy(a, b, sem.at[n]) for n, (a, b) in enumerate(pairs)]
    for copy in started:
        copy.start()
    for copy in started:
        copy.wait()


def pack_kernel(q_ref, k_ref, v_ref, do_ref, seg_ref, out_ref, seg_s, sem):
    pairs = [(seg_ref, seg_s)]
    for m in range(CHIPS):
        for part in range(2):
            at = pl.ds(part * ROWS, ROWS)
            pairs.append((q_ref.at[:, columns(2 * m + part)], out_ref.at[m, at, :]))
            at = pl.ds(DO_AT + part * ROWS, ROWS)
            pairs.append((do_ref.at[:, columns(2 * m + part)], out_ref.at[m, at, :]))
        pairs.append((k_ref.at[:, columns(m)], out_ref.at[m, pl.ds(KV_AT, ROWS), :]))
        pairs.append((v_ref.at[:, columns(m)], out_ref.at[m, pl.ds(KV_AT + ROWS, ROWS), :]))

    run_copies(pairs, sem)
    seg = jnp.broadcast_to(seg_s[...].astype(jnp.float32), (SEG_ROWS, ROWS))
    for m in range(CHIPS):
        out_ref[m, KV_AT + 2 * ROWS :, :] = seg.astype(jnp.bfloat16)


def unpack_kernel(in_ref, dq_ref, dk_ref, dv_ref, sem):
    pairs = []
    for m in range(CHIPS):
        for part in range(2):
            pairs.append((in_ref.at[m, pl.ds(part * ROWS, ROWS), :], dq_ref.at[:, columns(2 * m + part)]))
        pairs.append((in_ref.at[m, pl.ds(PAIR, ROWS), :], dk_ref.at[:, columns(m)]))
        pairs.append((in_ref.at[m, pl.ds(PAIR + ROWS, ROWS), :], dv_ref.at[:, columns(m)]))
    run_copies(pairs, sem)


def main_kernel(
    core_ref, in_ref, other_ref, dq_ref, keep_ref, send_ref,
    k_s, v_s, kt_s, first_s, low_s, dk_s, dv_s, e_s, g_s, dp_s, p_s, ds_s,
):
    core = core_ref[0]
    seg_rows = []
    for n in range(CHIPS):
        for which, ref, at in ((core, in_ref, KV_AT), (1 - core, other_ref, 0)):
            rows = pl.ds(pl.multiple_of(n * PAIR + which * ROWS, ROWS), ROWS)
            key = ref[n, at : at + ROWS, :]
            k_s[rows, :] = key
            v_s[rows, :] = ref[n, at + ROWS : at + 2 * ROWS, :]
            kt_s[:, rows] = key.T
        mine = in_ref[n, KV_AT + 2 * ROWS :, :][:1].astype(jnp.float32)
        theirs = other_ref[n, 2 * ROWS :, :][:1].astype(jnp.float32)
        seg_rows.append((mine, theirs))
    dk_s[...] = jnp.zeros_like(dk_s)
    dv_s[...] = jnp.zeros_like(dv_s)

    mine = jnp.concatenate([a for a, _ in seg_rows], axis=0)
    theirs = jnp.concatenate([b for _, b in seg_rows], axis=0)
    first = jnp.zeros_like(mine)
    for d in range(1, DOCS):
        below = jnp.where(mine < float(d), 1.0, 0.0) + jnp.where(theirs < float(d), 1.0, 0.0)
        start = jnp.sum(jnp.sum(below, axis=1, keepdims=True), axis=0, keepdims=True)
        first = jnp.where(mine == float(d), start, first)
    first = first.astype(jnp.int32)
    first_s[:, 0:ROWS] = first
    first_s[:, ROWS:] = first
    for n in range(CHIPS):
        low_s[n] = jnp.min(first[n : n + 1, :]) // ROWS

    def one_block(n, low, width):
        q = in_ref[n, 0:PAIR, :]
        do = in_ref[n, DO_AT : DO_AT + PAIR, :]
        start = first_s[pl.ds(n, 1), :]
        key_at = lax.broadcasted_iota(jnp.int32, (ROWS, PAIR), 0)
        query_at = lax.broadcasted_iota(jnp.int32, (ROWS, PAIR), 1) % ROWS
        total = jnp.zeros((8, PAIR), jnp.float32)
        delta = jnp.zeros((8, PAIR), jnp.float32)
        for j in range(width):
            rows = pl.ds(pl.multiple_of((low + j) * ROWS, ROWS), ROWS)
            at = pl.ds(j * ROWS, ROWS)
            raw = lax.dot_general(k_s[rows, :], q, NT, preferred_element_type=jnp.float32)
            dprob = lax.dot_general(v_s[rows, :], do, NT, preferred_element_type=jnp.float32)
            capped = jnp.tanh(raw * to_cap)
            expo = jnp.exp2(capped * cap_log2)
            visible = key_at >= start - (low + j) * ROWS
            if j == width - 1:
                visible = visible & (key_at <= query_at)
            expo = jnp.where(visible, expo, 0.0)
            total += jnp.sum(expo.reshape(ROWS // 8, 8, PAIR), axis=0)
            delta += jnp.sum((expo * dprob).reshape(ROWS // 8, 8, PAIR), axis=0)
            e_s[at, :] = expo
            g_s[at, :] = expo * (1.0 - capped * capped)
            dp_s[at, :] = dprob
        inverse = 1.0 / jnp.sum(total, axis=0, keepdims=True)
        delta = jnp.sum(delta, axis=0, keepdims=True) * inverse
        for j in range(width):
            at = pl.ds(j * ROWS, ROWS)
            p_s[at, :] = (e_s[at, :] * inverse).astype(jnp.bfloat16)
            ds_s[at, :] = (g_s[at, :] * ((dp_s[at, :] - delta) * inverse)).astype(jnp.bfloat16)
        keys = width * ROWS
        rows = pl.ds(pl.multiple_of(low * ROWS, ROWS), keys)
        dscore = ds_s[0:keys, :]
        dv_s[rows, :] += jnp.dot(p_s[0:keys, :], do, preferred_element_type=jnp.float32)
        dk_s[rows, :] += jnp.dot(dscore, q, preferred_element_type=jnp.float32)
        dq = jnp.dot(kt_s[:, rows], dscore, preferred_element_type=jnp.float32)
        dq_ref[n] = (dq * score_scale).T.astype(jnp.bfloat16)

    @pl.loop(0, CHIPS)
    def _(n):
        low = low_s[n]
        for width in range(1, WIDEST + 1):

            @pl.when(2 * n + core + 1 - low == width)
            def _():
                one_block(n, low, width)

    for n in range(CHIPS):
        for which, ref in ((core, keep_ref), (1 - core, send_ref)):
            rows = pl.ds(pl.multiple_of(n * PAIR + which * ROWS, ROWS), ROWS)
            ref[n, 0:ROWS, :] = (dk_s[rows, :] * score_scale).astype(jnp.bfloat16)
            ref[n, ROWS:, :] = dv_s[rows, :].astype(jnp.bfloat16)


def join_kernel(dq_ref, keep_ref, got_ref, out_ref):
    out_ref[:, 0:PAIR, :] = dq_ref[...]
    total = keep_ref[...].astype(jnp.float32) + got_ref[...].astype(jnp.float32)
    out_ref[:, PAIR:, :] = total.astype(jnp.bfloat16)


def call(kernel, out_shape, in_specs, out_specs, scratch, operands, flops=0):
    return pl.pallas_call(
        kernel,
        out_shape=out_shape,
        in_specs=in_specs,
        out_specs=out_specs,
        scratch_shapes=scratch,
        cost_estimate=pl.CostEstimate(flops=flops, bytes_accessed=1 << 20, transcendentals=0),
        compiler_params=pltpu.CompilerParams(vmem_limit_bytes=VMEM_LIMIT),
    )(*operands)


def main(core, first, other):
    return call(
        main_kernel,
        (bf16(CHIPS, PAIR, HEAD_SIZE),) * 3,
        [SMEM, VMEM, VMEM], (VMEM,) * 3,
        [
            pltpu.VMEM((TOKENS, HEAD_SIZE), jnp.bfloat16),
            pltpu.VMEM((TOKENS, HEAD_SIZE), jnp.bfloat16),
            pltpu.VMEM((HEAD_SIZE, TOKENS), jnp.bfloat16),
            pltpu.VMEM((CHIPS, PAIR), jnp.int32),
            pltpu.SMEM((CHIPS,), jnp.int32),
            pltpu.VMEM((TOKENS, HEAD_SIZE), jnp.float32),
            pltpu.VMEM((TOKENS, HEAD_SIZE), jnp.float32),
            pltpu.VMEM((WIDEST * ROWS, PAIR), jnp.float32),
            pltpu.VMEM((WIDEST * ROWS, PAIR), jnp.float32),
            pltpu.VMEM((WIDEST * ROWS, PAIR), jnp.float32),
            pltpu.VMEM((WIDEST * ROWS, PAIR), jnp.bfloat16),
            pltpu.VMEM((WIDEST * ROWS, PAIR), jnp.bfloat16),
        ],
        (core, first, other),
        flops=1 << 32,
    )


def body(queries, keys, values, dout, segments):
    swap = [(i, i ^ 1) for i in range(CHIPS * CORES)]
    planes = [[CORES * n + c for n in range(CHIPS)] for c in range(CORES)]
    core = (lax.axis_index("blk") % CORES).astype(jnp.int32).reshape(1)
    packed = call(
        pack_kernel, bf16(CHIPS, IN_ROWS, HEAD_SIZE), [HBM] * 5, VMEM,
        [pltpu.VMEM((1, ROWS), jnp.int32), pltpu.SemaphoreType.DMA((6 * CHIPS + 1,))],
        [
            pltpu.with_memory_space_constraint(a, pltpu.HBM)
            for a in (queries, keys, values, dout, segments.reshape(1, ROWS))
        ],
    )
    first = lax.all_to_all(packed, "blk", 0, 0, tiled=True, axis_index_groups=planes)
    other = lax.ppermute(first[:, KV_AT:, :], "blk", swap)
    dq, keep, send = main(core, first, other)
    got = lax.ppermute(send, "blk", swap)
    joined = call(
        join_kernel, bf16(CHIPS, 2 * PAIR, HEAD_SIZE), [VMEM] * 3, VMEM, [], (dq, keep, got)
    )
    back = lax.all_to_all(joined, "blk", 0, 0, tiled=True, axis_index_groups=planes)
    narrow = bf16(ROWS, CHIPS * HEAD_SIZE)
    return call(
        unpack_kernel, (bf16(ROWS, 2 * CHIPS * HEAD_SIZE), narrow, narrow), [VMEM], (HBM,) * 3,
        [pltpu.SemaphoreType.DMA((4 * CHIPS,))], (back,),
    )


def solution(mesh):
    rows = P(("grp", "blk"), None)
    in_specs = (rows, rows, rows, rows, P(("grp", "blk")))
    return jax.shard_map(body, mesh=mesh, in_specs=in_specs, out_specs=(rows, rows, rows), check_vma=False)
```

```python
import math
import jax
import jax.numpy as jnp
from jax import lax
from jax.experimental import pallas as pl
from jax.experimental.pallas import tpu as pltpu
from jax.sharding import PartitionSpec as P

HEAD_SIZE = 128
DOCS = 8
CHIPS = 8
CORES = 2
ROWS = 128
PAIR = CORES * ROWS
SEG_ROWS = 16
DO_AT = PAIR
KV_AT = 2 * PAIR
KV_ROWS = 2 * ROWS + SEG_ROWS
IN_ROWS = KV_AT + KV_ROWS
TOKENS = CHIPS * PAIR
WIDEST = 9
AHEAD = WIDEST - 1
AT_ONCE = 2

score_scale = 1.0 / 12.0
cap_value = 50.0
to_cap = score_scale / cap_value
cap_log2 = cap_value * math.log2(math.e)

NT = (((1,), (1,)), ((), ()))
TN = (((0,), (0,)), ((), ()))
VMEM_LIMIT = 32 * 1024 * 1024

ANY = pl.BlockSpec(memory_space=pl.ANY)
HBM = pl.BlockSpec(memory_space=pltpu.HBM)
VMEM = pl.BlockSpec(memory_space=pltpu.VMEM)
SMEM = pl.BlockSpec(memory_space=pltpu.SMEM)


def bf16(*shape):
    return jax.ShapeDtypeStruct(shape, jnp.bfloat16)


def columns(h):
    return pl.ds(h * HEAD_SIZE, HEAD_SIZE)


def key_rows(block, blocks=1):
    return pl.ds(pl.multiple_of((AHEAD + block) * ROWS, ROWS), blocks * ROWS)


def run_copies(pairs, sem):
    started = [pltpu.make_async_copy(a, b, sem.at[n]) for n, (a, b) in enumerate(pairs)]
    for copy in started:
        copy.start()
    for copy in started:
        copy.wait()


def pack_kernel(q_ref, k_ref, v_ref, do_ref, seg_ref, out_ref, seg_s, sem):
    pairs = [(seg_ref, seg_s)]
    for m in range(CHIPS):
        for part in range(2):
            at = pl.ds(part * ROWS, ROWS)
            pairs.append((q_ref.at[:, columns(2 * m + part)], out_ref.at[m, at, :]))
            at = pl.ds(DO_AT + part * ROWS, ROWS)
            pairs.append((do_ref.at[:, columns(2 * m + part)], out_ref.at[m, at, :]))
        pairs.append((k_ref.at[:, columns(m)], out_ref.at[m, pl.ds(KV_AT, ROWS), :]))
        pairs.append((v_ref.at[:, columns(m)], out_ref.at[m, pl.ds(KV_AT + ROWS, ROWS), :]))

    run_copies(pairs, sem)
    seg = jnp.broadcast_to(seg_s[...].astype(jnp.float32), (SEG_ROWS, ROWS))
    for m in range(CHIPS):
        out_ref[m, KV_AT + 2 * ROWS :, :] = seg.astype(jnp.bfloat16)


def unpack_kernel(in_ref, dq_ref, dk_ref, dv_ref, sem):
    pairs = []
    for m in range(CHIPS):
        for part in range(2):
            pairs.append((in_ref.at[m, pl.ds(part * ROWS, ROWS), :], dq_ref.at[:, columns(2 * m + part)]))
        pairs.append((in_ref.at[m, pl.ds(PAIR, ROWS), :], dk_ref.at[:, columns(m)]))
        pairs.append((in_ref.at[m, pl.ds(PAIR + ROWS, ROWS), :], dv_ref.at[:, columns(m)]))
    run_copies(pairs, sem)


def main_kernel(
    core_ref, in_ref, other_ref, dq_ref, keep_ref, send_ref,
    k_s, v_s, first_s, width_s, order_s, dk_s, dv_s, *work,
):
    core = core_ref[0]
    seg_rows = []
    for n in range(CHIPS):
        for which, ref, at in ((core, in_ref, KV_AT), (1 - core, other_ref, 0)):
            rows = key_rows(2 * n + which)
            k_s[rows, :] = ref[n, at : at + ROWS, :]
            v_s[rows, :] = ref[n, at + ROWS : at + 2 * ROWS, :]
        mine = in_ref[n, KV_AT + 2 * ROWS :, :][:1].astype(jnp.float32)
        theirs = other_ref[n, 2 * ROWS :, :][:1].astype(jnp.float32)
        seg_rows.append((mine, theirs))
    k_s[0 : AHEAD * ROWS, :] = jnp.zeros((AHEAD * ROWS, HEAD_SIZE), jnp.bfloat16)
    v_s[0 : AHEAD * ROWS, :] = jnp.zeros((AHEAD * ROWS, HEAD_SIZE), jnp.bfloat16)
    dk_s[AHEAD * ROWS :, :] = jnp.zeros((TOKENS, HEAD_SIZE), jnp.float32)
    dv_s[AHEAD * ROWS :, :] = jnp.zeros((TOKENS, HEAD_SIZE), jnp.float32)

    mine = jnp.concatenate([a for a, _ in seg_rows], axis=0)
    theirs = jnp.concatenate([b for _, b in seg_rows], axis=0)
    first = jnp.zeros_like(mine)
    for d in range(1, DOCS):
        below = jnp.where(mine < float(d), 1.0, 0.0) + jnp.where(theirs < float(d), 1.0, 0.0)
        start = jnp.sum(jnp.sum(below, axis=1, keepdims=True), axis=0, keepdims=True)
        first = jnp.where(mine == float(d), start, first)
    first = first.astype(jnp.int32)
    first_s[:, 0:ROWS] = first
    first_s[:, ROWS:] = first

    widths = [2 * n + core + 1 - jnp.min(first[n : n + 1, :]) // ROWS for n in range(CHIPS)]
    for n in range(CHIPS):
        before = [widths[m] <= widths[n] if m < n else widths[m] < widths[n] for m in range(CHIPS) if m != n]
        rank = sum(x.astype(jnp.int32) for x in before)
        order_s[rank] = n
        width_s[rank] = widths[n]

    def tiles_at_once(first_at, width):
        keys = width * ROWS
        tiles = [order_s[first_at + u] for u in range(AT_ONCE)]
        low = [2 * n + core + 1 - width for n in tiles]
        q = [in_ref[n, 0:PAIR, :] for n in tiles]
        do = [in_ref[n, DO_AT : DO_AT + PAIR, :] for n in tiles]
        start = [first_s[pl.ds(n, 1), :] for n in tiles]
        key_at = lax.broadcasted_iota(jnp.int32, (ROWS, PAIR), 0)
        query_at = lax.broadcasted_iota(jnp.int32, (ROWS, PAIR), 1) % ROWS
        total = [jnp.zeros((8, PAIR), jnp.float32) for _ in tiles]
        delta = [jnp.zeros((8, PAIR), jnp.float32) for _ in tiles]
        for j in range(width):
            at = pl.ds(j * ROWS, ROWS)
            for u in range(AT_ONCE):
                e_s, g_s, dp_s, _, _ = work[5 * u : 5 * u + 5]
                rows = key_rows(low[u] + j)
                raw = lax.dot_general(k_s[rows, :], q[u], NT, preferred_element_type=jnp.float32)
                dprob = lax.dot_general(v_s[rows, :], do[u], NT, preferred_element_type=jnp.float32)
                capped = jnp.tanh(raw * to_cap)
                expo = jnp.exp2(capped * cap_log2)
                visible = key_at >= start[u] - (low[u] + j) * ROWS
                if j == width - 1:
                    visible = visible & (key_at <= query_at)
                expo = jnp.where(visible, expo, 0.0)
                total[u] += jnp.sum(expo.reshape(ROWS // 8, 8, PAIR), axis=0)
                delta[u] += jnp.sum((expo * dprob).reshape(ROWS // 8, 8, PAIR), axis=0)
                e_s[at, :] = expo
                g_s[at, :] = expo * (1.0 - capped * capped)
                dp_s[at, :] = dprob
        inverse = [1.0 / jnp.sum(x, axis=0, keepdims=True) for x in total]
        delta = [jnp.sum(x, axis=0, keepdims=True) * y for x, y in zip(delta, inverse)]
        for u in range(AT_ONCE):
            e_s, g_s, dp_s, p_s, ds_s = work[5 * u : 5 * u + 5]
            for j in range(width):
                at = pl.ds(j * ROWS, ROWS)
                p_s[at, :] = (e_s[at, :] * inverse[u]).astype(jnp.bfloat16)
                ds_s[at, :] = (g_s[at, :] * ((dp_s[at, :] - delta[u]) * inverse[u])).astype(jnp.bfloat16)
        for u in range(AT_ONCE):
            _, _, _, p_s, ds_s = work[5 * u : 5 * u + 5]
            rows = key_rows(low[u], width)
            dscore = ds_s[0:keys, :]
            dv_s[rows, :] += jnp.dot(p_s[0:keys, :], do[u], preferred_element_type=jnp.float32)
            dk_s[rows, :] += jnp.dot(dscore, q[u], preferred_element_type=jnp.float32)
            dq = lax.dot_general(dscore, k_s[rows, :], TN, preferred_element_type=jnp.float32)
            dq_ref[tiles[u]] = (dq * score_scale).astype(jnp.bfloat16)

    @pl.loop(0, CHIPS // AT_ONCE)
    def _(group):
        first_at = group * AT_ONCE
        widest = width_s[first_at + AT_ONCE - 1]

        def choose(least, most):
            if least == most:
                tiles_at_once(first_at, least)
                return
            middle = (least + most) // 2

            @pl.when(widest <= middle)
            def _():
                choose(least, middle)

            @pl.when(widest > middle)
            def _():
                choose(middle + 1, most)

        choose(1, WIDEST)

    for n in range(CHIPS):
        for which, ref in ((core, keep_ref), (1 - core, send_ref)):
            rows = key_rows(2 * n + which)
            ref[n, 0:ROWS, :] = (dk_s[rows, :] * score_scale).astype(jnp.bfloat16)
            ref[n, ROWS:, :] = dv_s[rows, :].astype(jnp.bfloat16)


def join_kernel(dq_ref, keep_ref, got_ref, out_ref):
    out_ref[:, 0:PAIR, :] = dq_ref[...]
    total = keep_ref[...].astype(jnp.float32) + got_ref[...].astype(jnp.float32)
    out_ref[:, PAIR:, :] = total.astype(jnp.bfloat16)


def call(kernel, out_shape, in_specs, out_specs, scratch, operands, flops=0):
    return pl.pallas_call(
        kernel,
        out_shape=out_shape,
        in_specs=in_specs,
        out_specs=out_specs,
        scratch_shapes=scratch,
        cost_estimate=pl.CostEstimate(flops=flops, bytes_accessed=1 << 20, transcendentals=0),
        compiler_params=pltpu.CompilerParams(vmem_limit_bytes=VMEM_LIMIT),
    )(*operands)


def main(core, first, other):
    rows = (AHEAD * ROWS) + TOKENS
    seen = (WIDEST * ROWS, PAIR)
    return call(
        main_kernel,
        (bf16(CHIPS, PAIR, HEAD_SIZE),) * 3,
        [SMEM, VMEM, VMEM], (VMEM,) * 3,
        [
            pltpu.VMEM((rows, HEAD_SIZE), jnp.bfloat16),
            pltpu.VMEM((rows, HEAD_SIZE), jnp.bfloat16),
            pltpu.VMEM((CHIPS, PAIR), jnp.int32),
            pltpu.SMEM((CHIPS,), jnp.int32),
            pltpu.SMEM((CHIPS,), jnp.int32),
            pltpu.VMEM((rows, HEAD_SIZE), jnp.float32),
            pltpu.VMEM((rows, HEAD_SIZE), jnp.float32),
        ]
        + [
            pltpu.VMEM(seen, jnp.float32),
            pltpu.VMEM(seen, jnp.float32),
            pltpu.VMEM(seen, jnp.float32),
            pltpu.VMEM(seen, jnp.bfloat16),
            pltpu.VMEM(seen, jnp.bfloat16),
        ]
        * AT_ONCE,
        (core, first, other),
        flops=1 << 32,
    )


def body(queries, keys, values, dout, segments):
    swap = [(i, i ^ 1) for i in range(CHIPS * CORES)]
    planes = [[CORES * n + c for n in range(CHIPS)] for c in range(CORES)]
    core = (lax.axis_index("blk") % CORES).astype(jnp.int32).reshape(1)
    packed = call(
        pack_kernel, bf16(CHIPS, IN_ROWS, HEAD_SIZE), [HBM] * 5, VMEM,
        [pltpu.VMEM((1, ROWS), jnp.int32), pltpu.SemaphoreType.DMA((6 * CHIPS + 1,))],
        [
            pltpu.with_memory_space_constraint(a, pltpu.HBM)
            for a in (queries, keys, values, dout, segments.reshape(1, ROWS))
        ],
    )
    first = lax.all_to_all(packed, "blk", 0, 0, tiled=True, axis_index_groups=planes)
    other = lax.ppermute(first[:, KV_AT:, :], "blk", swap)
    dq, keep, send = main(core, first, other)
    got = lax.ppermute(send, "blk", swap)
    joined = call(
        join_kernel, bf16(CHIPS, 2 * PAIR, HEAD_SIZE), [VMEM] * 3, VMEM, [], (dq, keep, got)
    )
    back = lax.all_to_all(joined, "blk", 0, 0, tiled=True, axis_index_groups=planes)
    narrow = bf16(ROWS, CHIPS * HEAD_SIZE)
    return call(
        unpack_kernel, (bf16(ROWS, 2 * CHIPS * HEAD_SIZE), narrow, narrow), [VMEM], (HBM,) * 3,
        [pltpu.SemaphoreType.DMA((4 * CHIPS,))], (back,),
    )


def solution(mesh):
    rows = P(("grp", "blk"), None)
    in_specs = (rows, rows, rows, rows, P(("grp", "blk")))
    return jax.shard_map(body, mesh=mesh, in_specs=in_specs, out_specs=(rows, rows, rows), check_vma=False)
```

```python
import functools
import math
import jax
import jax.numpy as jnp
from jax import lax
from jax.experimental import pallas as pl
from jax.experimental.pallas import tpu as pltpu
from jax.sharding import PartitionSpec as P

HEAD_SIZE = 128
DOCS = 8
CHIPS = 8
CORES = 2
ROWS = 128
PAIR = CORES * ROWS
SEG_ROWS = 16
DO_AT = PAIR
KV_AT = 2 * PAIR
KV_ROWS = 2 * ROWS + SEG_ROWS
IN_ROWS = KV_AT + KV_ROWS
TOKENS = CHIPS * PAIR
WIDEST = 9
REACH = 4
AT_ONCE = 2

score_scale = 1.0 / 12.0
cap_value = 50.0
to_cap = score_scale / cap_value
cap_log2 = cap_value * math.log2(math.e)

NT = (((1,), (1,)), ((), ()))
TN = (((0,), (0,)), ((), ()))
VMEM_LIMIT = 32 * 1024 * 1024

ANY = pl.BlockSpec(memory_space=pl.ANY)
HBM = pl.BlockSpec(memory_space=pltpu.HBM)
VMEM = pl.BlockSpec(memory_space=pltpu.VMEM)
SMEM = pl.BlockSpec(memory_space=pltpu.SMEM)


def bf16(*shape):
    return jax.ShapeDtypeStruct(shape, jnp.bfloat16)


def columns(h):
    return pl.ds(h * HEAD_SIZE, HEAD_SIZE)


def pack_kernel(q_ref, k_ref, v_ref, do_ref, seg_ref, out_ref, q_s, k_s, v_s, do_s, seg_s, sem):
    held = (q_s, do_s, k_s, v_s, seg_s)
    copies = [
        pltpu.make_async_copy(a, b, sem.at[n])
        for n, (a, b) in enumerate(zip((q_ref, do_ref, k_ref, v_ref, seg_ref), held))
    ]
    for copy in copies:
        copy.start()
    for copy, ref, at in zip(copies, held, (0, DO_AT)):
        copy.wait()
        for m in range(CHIPS):
            for part in range(2):
                out_ref[m, at + part * ROWS : at + (part + 1) * ROWS, :] = ref[:, columns(2 * m + part)]
    for copy, ref, at in zip(copies[2:], held[2:], (KV_AT, KV_AT + ROWS)):
        copy.wait()
        for m in range(CHIPS):
            out_ref[m, at : at + ROWS, :] = ref[:, columns(m)]
    copies[-1].wait()
    seg = jnp.broadcast_to(seg_s[...].astype(jnp.float32), (SEG_ROWS, ROWS))
    for m in range(CHIPS):
        out_ref[m, KV_AT + 2 * ROWS :, :] = seg.astype(jnp.bfloat16)


def unpack_kernel(in_ref, dq_ref, dk_ref, dv_ref, dq_s, dk_s, dv_s, sem):
    started = []

    def send(held, out):
        started.append(pltpu.make_async_copy(held, out, sem.at[len(started)]))
        started[-1].start()

    for m in range(CHIPS):
        for part in range(2):
            dq_s[:, columns(2 * m + part)] = in_ref[m, part * ROWS : (part + 1) * ROWS, :]
    send(dq_s, dq_ref)
    for held, out, at in ((dk_s, dk_ref, PAIR), (dv_s, dv_ref, PAIR + ROWS)):
        for m in range(CHIPS):
            held[:, columns(m)] = in_ref[m, at : at + ROWS, :]
        send(held, out)
    for copy in started:
        copy.wait()


def seen_blocks(n, core, width, in_ref, other_ref):
    for i in range(width):
        if i % 2 == 0:
            chip, ref, at = jnp.maximum(n - i // 2, 0), in_ref, KV_AT
        else:
            chip, ref, at = jnp.maximum(n - (i + 1) // 2 + core, 0), other_ref, 0
        yield i, 2 * n + core - i, chip, ref.at[chip, pl.ds(at, ROWS)], ref.at[chip, pl.ds(at + ROWS, ROWS)]


def by_width(width, case):
    def choose(least, most):
        if least == most:
            case(least)
            return
        middle = (least + most) // 2

        @pl.when(width <= middle)
        def _():
            choose(least, middle)

        @pl.when(width > middle)
        def _():
            choose(middle + 1, most)

    choose(1, WIDEST)


def main_kernel(
    core_ref, in_ref, other_ref, dq_ref, keep_ref, send_ref, order_ref, width_ref, first_s, *work
):
    core = core_ref[0]
    dk_s, dv_s, work = work[0:2], work[2:4], work[4:]
    for sum_s in (*dk_s, *dv_s):
        sum_s[REACH : REACH + CHIPS] = jnp.zeros((CHIPS, ROWS, HEAD_SIZE), jnp.float32)

    mine = jnp.concatenate(
        [in_ref[n, KV_AT + 2 * ROWS :, :][:1].astype(jnp.float32) for n in range(CHIPS)], axis=0
    )
    theirs = jnp.concatenate([other_ref[n, 2 * ROWS :, :][:1].astype(jnp.float32) for n in range(CHIPS)], axis=0)
    first = jnp.zeros_like(mine)
    for d in range(1, DOCS):
        below = jnp.where(mine < float(d), 1.0, 0.0) + jnp.where(theirs < float(d), 1.0, 0.0)
        start = jnp.sum(jnp.sum(below, axis=1, keepdims=True), axis=0, keepdims=True)
        first = jnp.where(mine == float(d), start, first)
    first = first.astype(jnp.int32)
    first_s[:, 0:ROWS] = first
    first_s[:, ROWS:] = first

    widths = [2 * n + core + 1 - jnp.min(first[n : n + 1, :]) // ROWS for n in range(CHIPS)]
    for n in range(CHIPS):
        before = [widths[m] <= widths[n] if m < n else widths[m] < widths[n] for m in range(CHIPS) if m != n]
        rank = sum(x.astype(jnp.int32) for x in before)
        order_ref[rank] = n
        width_ref[rank] = widths[n]

    def tiles_at_once(first_at, width):
        tiles = [order_ref[first_at + u] for u in range(AT_ONCE)]
        q = [in_ref[n, 0:PAIR, :] for n in tiles]
        do = [in_ref[n, DO_AT : DO_AT + PAIR, :] for n in tiles]
        start = [first_s[pl.ds(n, 1), :] for n in tiles]
        seen = [list(seen_blocks(n, core, width, in_ref, other_ref)) for n in tiles]
        key_at = lax.broadcasted_iota(jnp.int32, (ROWS, PAIR), 0)
        query_at = lax.broadcasted_iota(jnp.int32, (ROWS, PAIR), 1) % ROWS
        total = [jnp.zeros((8, PAIR), jnp.float32) for _ in tiles]
        delta = [jnp.zeros((8, PAIR), jnp.float32) for _ in tiles]
        for j in range(width):
            at = pl.ds(j * ROWS, ROWS)
            for u in range(AT_ONCE):
                e_s, g_s, dp_s = work[3 * u : 3 * u + 3]
                _, block, _, k, v = seen[u][j]
                raw = lax.dot_general(k[...], q[u], NT, preferred_element_type=jnp.float32)
                dprob = lax.dot_general(v[...], do[u], NT, preferred_element_type=jnp.float32)
                capped = jnp.tanh(raw * to_cap)
                expo = jnp.exp2(capped * cap_log2)
                visible = key_at >= start[u] - block * ROWS
                if j == 0:
                    visible = visible & (key_at <= query_at)
                expo = jnp.where(visible, expo, 0.0)
                total[u] += jnp.sum(expo.reshape(ROWS // 8, 8, PAIR), axis=0)
                delta[u] += jnp.sum((expo * dprob).reshape(ROWS // 8, 8, PAIR), axis=0)
                e_s[at, :] = expo
                g_s[at, :] = 1.0 - capped * capped
                dp_s[at, :] = dprob
        dscores = [[] for _ in tiles]
        inverse = [1.0 / jnp.sum(x, axis=0, keepdims=True) for x in total]
        delta = [jnp.sum(x, axis=0, keepdims=True) * y for x, y in zip(delta, inverse)]
        for u in range(AT_ONCE):
            e_s, g_s, dp_s = work[3 * u : 3 * u + 3]
            for j in range(width):
                at = pl.ds(j * ROWS, ROWS)
                prob = e_s[at, :] * inverse[u]
                low = prob.astype(jnp.bfloat16)
                dscore = (prob * (dp_s[at, :] - delta[u]) * g_s[at, :]).astype(jnp.bfloat16)
                which = j % 2
                place = pl.ds(tiles[u] + (core if which else 0), REACH + 1)
                place = REACH - (j + 1) // 2, place
                dv_s[which].at[place[1]][place[0]] += jnp.dot(low, do[u], preferred_element_type=jnp.float32)
                dk_s[which].at[place[1]][place[0]] += jnp.dot(dscore, q[u], preferred_element_type=jnp.float32)
                dscores[u].append(dscore)
        for u in range(AT_ONCE):
            keys = jnp.concatenate([x[3][...] for x in seen[u]], axis=0)
            dscore = jnp.concatenate(dscores[u], axis=0)
            dq = lax.dot_general(dscore, keys, TN, preferred_element_type=jnp.float32)
            dq_ref[tiles[u]] = (dq * score_scale).astype(jnp.bfloat16)

    @pl.loop(0, CHIPS // AT_ONCE)
    def _(group):
        first_at = group * AT_ONCE
        by_width(width_ref[first_at + AT_ONCE - 1], functools.partial(tiles_at_once, first_at))

    for ref, dk, dv in zip((keep_ref, send_ref), dk_s, dv_s):
        ref[:, 0:ROWS, :] = (dk[REACH : REACH + CHIPS] * score_scale).astype(jnp.bfloat16)
        ref[:, ROWS:, :] = dv[REACH : REACH + CHIPS].astype(jnp.bfloat16)


def join_kernel(dq_ref, keep_ref, got_ref, out_ref):
    out_ref[:, 0:PAIR, :] = dq_ref[...]
    total = keep_ref[...].astype(jnp.float32) + got_ref[...].astype(jnp.float32)
    out_ref[:, PAIR:, :] = total.astype(jnp.bfloat16)


def call(kernel, out_shape, in_specs, out_specs, scratch, operands, flops=0):
    return pl.pallas_call(
        kernel,
        out_shape=out_shape,
        in_specs=in_specs,
        out_specs=out_specs,
        scratch_shapes=scratch,
        cost_estimate=pl.CostEstimate(flops=flops, bytes_accessed=1 << 20, transcendentals=0),
        compiler_params=pltpu.CompilerParams(vmem_limit_bytes=VMEM_LIMIT),
    )(*operands)


def main(core, first, other):
    half = bf16(CHIPS, PAIR, HEAD_SIZE)
    return call(
        main_kernel, (half, half, half),
        [SMEM, VMEM, VMEM], (VMEM, VMEM, VMEM),
        [pltpu.SMEM((CHIPS,), jnp.int32)] * 2
        + [pltpu.VMEM((CHIPS, PAIR), jnp.int32)]
        + [pltpu.VMEM((REACH + CHIPS + 1, ROWS, HEAD_SIZE), jnp.float32)] * 4
        + [pltpu.VMEM((WIDEST * ROWS, PAIR), jnp.float32)] * (3 * AT_ONCE),
        (core, first, other),
        flops=1 << 32,
    )


def body(queries, keys, values, dout, segments):
    swap = [(i, i ^ 1) for i in range(CHIPS * CORES)]
    planes = [[CORES * n + c for n in range(CHIPS)] for c in range(CORES)]
    core = (lax.axis_index("blk") % CORES).astype(jnp.int32).reshape(1)
    packed = call(
        pack_kernel, bf16(CHIPS, IN_ROWS, HEAD_SIZE), [HBM] * 5, VMEM,
        [
            pltpu.VMEM((ROWS, 2 * CHIPS * HEAD_SIZE), jnp.bfloat16),
            pltpu.VMEM((ROWS, CHIPS * HEAD_SIZE), jnp.bfloat16),
            pltpu.VMEM((ROWS, CHIPS * HEAD_SIZE), jnp.bfloat16),
            pltpu.VMEM((ROWS, 2 * CHIPS * HEAD_SIZE), jnp.bfloat16),
            pltpu.VMEM((1, ROWS), jnp.int32),
            pltpu.SemaphoreType.DMA((5,)),
        ],
        [
            pltpu.with_memory_space_constraint(a, pltpu.HBM)
            for a in (queries, keys, values, dout, segments.reshape(1, ROWS))
        ],
    )
    first = lax.all_to_all(packed, "blk", 0, 0, tiled=True, axis_index_groups=planes)
    other = lax.ppermute(first[:, KV_AT:, :], "blk", swap)
    dq, keep, send = main(core, first, other)
    got = lax.ppermute(send, "blk", swap)
    joined = call(
        join_kernel, bf16(CHIPS, 2 * PAIR, HEAD_SIZE), [VMEM] * 3, VMEM, [], (dq, keep, got)
    )
    back = lax.all_to_all(joined, "blk", 0, 0, tiled=True, axis_index_groups=planes)
    narrow = bf16(ROWS, CHIPS * HEAD_SIZE)
    return call(
        unpack_kernel, (bf16(ROWS, 2 * CHIPS * HEAD_SIZE), narrow, narrow), [VMEM], (HBM,) * 3,
        [
            pltpu.VMEM((ROWS, 2 * CHIPS * HEAD_SIZE), jnp.bfloat16),
            pltpu.VMEM((ROWS, CHIPS * HEAD_SIZE), jnp.bfloat16),
            pltpu.VMEM((ROWS, CHIPS * HEAD_SIZE), jnp.bfloat16),
            pltpu.SemaphoreType.DMA((3,)),
        ],
        (back,),
    )


def solution(mesh):
    rows = P(("grp", "blk"), None)
    in_specs = (rows, rows, rows, rows, P(("grp", "blk")))
    return jax.shard_map(body, mesh=mesh, in_specs=in_specs, out_specs=(rows, rows, rows), check_vma=False)
```

```python
import functools
import math
import jax
import jax.numpy as jnp
from jax import lax
from jax.experimental import pallas as pl
from jax.experimental.pallas import tpu as pltpu
from jax.sharding import PartitionSpec as P

HEAD_SIZE = 128
DOCS = 8
CHIPS = 8
CORES = 2
ROWS = 128
PAIR = CORES * ROWS
SEG_ROWS = 16
DO_AT = PAIR
KV_AT = 2 * PAIR
KV_ROWS = 2 * ROWS + SEG_ROWS
IN_ROWS = KV_AT + KV_ROWS
TOKENS = CHIPS * PAIR
WIDEST = 9
REACH = 4
LESS = 2
AT_ONCE = 2

score_scale = 1.0 / 12.0
cap_value = 50.0
to_cap = score_scale / cap_value
cap_log2 = cap_value * math.log2(math.e)

NT = (((1,), (1,)), ((), ()))
TN = (((0,), (0,)), ((), ()))
VMEM_LIMIT = 32 * 1024 * 1024

ANY = pl.BlockSpec(memory_space=pl.ANY)
HBM = pl.BlockSpec(memory_space=pltpu.HBM)
VMEM = pl.BlockSpec(memory_space=pltpu.VMEM)
SMEM = pl.BlockSpec(memory_space=pltpu.SMEM)


def bf16(*shape):
    return jax.ShapeDtypeStruct(shape, jnp.bfloat16)


def columns(h):
    return pl.ds(h * HEAD_SIZE, HEAD_SIZE)


def pack_kernel(q_ref, k_ref, v_ref, do_ref, seg_ref, out_ref, q_s, k_s, v_s, do_s, seg_s, sem):
    held = (q_s, do_s, k_s, v_s, seg_s)
    copies = [
        pltpu.make_async_copy(a, b, sem.at[n])
        for n, (a, b) in enumerate(zip((q_ref, do_ref, k_ref, v_ref, seg_ref), held))
    ]
    for copy in copies:
        copy.start()
    for copy, ref, at in zip(copies, held, (0, DO_AT)):
        copy.wait()
        for m in range(CHIPS):
            for part in range(2):
                out_ref[m, at + part * ROWS : at + (part + 1) * ROWS, :] = ref[:, columns(2 * m + part)]
    for copy, ref, at in zip(copies[2:], held[2:], (KV_AT, KV_AT + ROWS)):
        copy.wait()
        for m in range(CHIPS):
            out_ref[m, at : at + ROWS, :] = ref[:, columns(m)]
    copies[-1].wait()
    seg = jnp.broadcast_to(seg_s[...].astype(jnp.float32), (SEG_ROWS, ROWS))
    for m in range(CHIPS):
        out_ref[m, KV_AT + 2 * ROWS :, :] = seg.astype(jnp.bfloat16)


def unpack_kernel(in_ref, dq_ref, dk_ref, dv_ref, dq_s, dk_s, dv_s, sem):
    started = []

    def send(held, out):
        started.append(pltpu.make_async_copy(held, out, sem.at[len(started)]))
        started[-1].start()

    for m in range(CHIPS):
        for part in range(2):
            dq_s[:, columns(2 * m + part)] = in_ref[m, part * ROWS : (part + 1) * ROWS, :]
    send(dq_s, dq_ref)
    for held, out, at in ((dk_s, dk_ref, PAIR), (dv_s, dv_ref, PAIR + ROWS)):
        for m in range(CHIPS):
            held[:, columns(m)] = in_ref[m, at : at + ROWS, :]
        send(held, out)
    for copy in started:
        copy.wait()


def seen_blocks(n, core, width, in_ref, other_ref):
    for i in range(width):
        if i % 2 == 0:
            chip, ref, at = jnp.maximum(n - i // 2, 0), in_ref, KV_AT
        else:
            chip, ref, at = jnp.maximum(n - (i + 1) // 2 + core, 0), other_ref, 0
        yield i, 2 * n + core - i, chip, ref.at[chip, pl.ds(at, ROWS)], ref.at[chip, pl.ds(at + ROWS, ROWS)]


def by_width(width, case):
    def choose(least, most):
        if least == most:
            case(least)
            return
        middle = (least + most) // 2

        @pl.when(width <= middle)
        def _():
            choose(least, middle)

        @pl.when(width > middle)
        def _():
            choose(middle + 1, most)

    choose(1, WIDEST)


def main_kernel(
    core_ref, in_ref, other_ref, dq_ref, keep_ref, send_ref, order_ref, width_ref, first_s, *work
):
    core = core_ref[0]
    dk_s, dv_s, work = work[0:2], work[2:4], work[4:]
    for sum_s in (*dk_s, *dv_s):
        sum_s[REACH : REACH + CHIPS] = jnp.zeros((CHIPS, ROWS, HEAD_SIZE), jnp.float32)

    mine = jnp.concatenate(
        [in_ref[n, KV_AT + 2 * ROWS :, :][:1].astype(jnp.float32) for n in range(CHIPS)], axis=0
    )
    theirs = jnp.concatenate([other_ref[n, 2 * ROWS :, :][:1].astype(jnp.float32) for n in range(CHIPS)], axis=0)
    first = jnp.zeros_like(mine)
    for d in range(1, DOCS):
        below = jnp.where(mine < float(d), 1.0, 0.0) + jnp.where(theirs < float(d), 1.0, 0.0)
        start = jnp.sum(jnp.sum(below, axis=1, keepdims=True), axis=0, keepdims=True)
        first = jnp.where(mine == float(d), start, first)
    first = first.astype(jnp.int32)
    first_s[:, 0:ROWS] = first
    first_s[:, ROWS:] = first

    widths = [2 * n + core + 1 - jnp.min(first[n : n + 1, :]) // ROWS for n in range(CHIPS)]
    for n in range(CHIPS):
        before = [widths[m] <= widths[n] if m < n else widths[m] < widths[n] for m in range(CHIPS) if m != n]
        rank = sum(x.astype(jnp.int32) for x in before)
        order_ref[rank] = n
        width_ref[rank] = widths[n]

    def tiles_at_once(first_at, less, width):
        widths = (width - less, width)
        tiles = [order_ref[first_at + u] for u in range(AT_ONCE)]
        q = [in_ref[n, 0:PAIR, :] for n in tiles]
        do = [in_ref[n, DO_AT : DO_AT + PAIR, :] for n in tiles]
        start = [first_s[pl.ds(n, 1), :] for n in tiles]
        seen = [list(seen_blocks(n, core, w, in_ref, other_ref)) for n, w in zip(tiles, widths)]
        key_at = lax.broadcasted_iota(jnp.int32, (ROWS, PAIR), 0)
        query_at = lax.broadcasted_iota(jnp.int32, (ROWS, PAIR), 1) % ROWS
        total = [jnp.zeros((8, PAIR), jnp.float32) for _ in tiles]
        delta = [jnp.zeros((8, PAIR), jnp.float32) for _ in tiles]
        for j in range(width):
            at = pl.ds(j * ROWS, ROWS)
            for u in range(AT_ONCE):
                if j >= widths[u]:
                    continue
                e_s, g_s, dp_s = work[3 * u : 3 * u + 3]
                _, block, _, k, v = seen[u][j]
                raw = lax.dot_general(k[...], q[u], NT, preferred_element_type=jnp.float32)
                dprob = lax.dot_general(v[...], do[u], NT, preferred_element_type=jnp.float32)
                capped = jnp.tanh(raw * to_cap)
                expo = jnp.exp2(capped * cap_log2)
                visible = key_at >= start[u] - block * ROWS
                if j == 0:
                    visible = visible & (key_at <= query_at)
                expo = jnp.where(visible, expo, 0.0)
                total[u] += jnp.sum(expo.reshape(ROWS // 8, 8, PAIR), axis=0)
                delta[u] += jnp.sum((expo * dprob).reshape(ROWS // 8, 8, PAIR), axis=0)
                e_s[at, :] = expo
                g_s[at, :] = 1.0 - capped * capped
                dp_s[at, :] = dprob
        dscores = [[] for _ in tiles]
        inverse = [1.0 / jnp.sum(x, axis=0, keepdims=True) for x in total]
        delta = [jnp.sum(x, axis=0, keepdims=True) * y for x, y in zip(delta, inverse)]
        for u in range(AT_ONCE):
            e_s, g_s, dp_s = work[3 * u : 3 * u + 3]
            for j in range(widths[u]):
                at = pl.ds(j * ROWS, ROWS)
                prob = e_s[at, :] * inverse[u]
                low = prob.astype(jnp.bfloat16)
                dscore = (prob * (dp_s[at, :] - delta[u]) * g_s[at, :]).astype(jnp.bfloat16)
                which = j % 2
                place = pl.ds(tiles[u] + (core if which else 0), REACH + 1)
                place = REACH - (j + 1) // 2, place
                dv_s[which].at[place[1]][place[0]] += jnp.dot(low, do[u], preferred_element_type=jnp.float32)
                dk_s[which].at[place[1]][place[0]] += jnp.dot(dscore, q[u], preferred_element_type=jnp.float32)
                dscores[u].append(dscore)
        for u in range(AT_ONCE):
            keys = jnp.concatenate([x[3][...] for x in seen[u]], axis=0)
            dscore = jnp.concatenate(dscores[u], axis=0)
            dq = lax.dot_general(dscore, keys, TN, preferred_element_type=jnp.float32)
            dq_ref[tiles[u]] = (dq * score_scale).astype(jnp.bfloat16)

    @pl.loop(0, CHIPS // AT_ONCE)
    def _(group):
        first_at = group * AT_ONCE
        widest = width_ref[first_at + 1]
        gap = widest - width_ref[first_at]

        def pair(width):
            if width <= LESS:
                tiles_at_once(first_at, 0, width)
                return

            @pl.when(gap < LESS)
            def _():
                tiles_at_once(first_at, 0, width)

            @pl.when(gap >= LESS)
            def _():
                tiles_at_once(first_at, LESS, width)

        by_width(widest, pair)

    for ref, dk, dv in zip((keep_ref, send_ref), dk_s, dv_s):
        ref[:, 0:ROWS, :] = (dk[REACH : REACH + CHIPS] * score_scale).astype(jnp.bfloat16)
        ref[:, ROWS:, :] = dv[REACH : REACH + CHIPS].astype(jnp.bfloat16)


def join_kernel(dq_ref, keep_ref, got_ref, out_ref):
    out_ref[:, 0:PAIR, :] = dq_ref[...]
    total = keep_ref[...].astype(jnp.float32) + got_ref[...].astype(jnp.float32)
    out_ref[:, PAIR:, :] = total.astype(jnp.bfloat16)


def call(kernel, out_shape, in_specs, out_specs, scratch, operands, flops=0):
    return pl.pallas_call(
        kernel,
        out_shape=out_shape,
        in_specs=in_specs,
        out_specs=out_specs,
        scratch_shapes=scratch,
        cost_estimate=pl.CostEstimate(flops=flops, bytes_accessed=1 << 20, transcendentals=0),
        compiler_params=pltpu.CompilerParams(vmem_limit_bytes=VMEM_LIMIT),
    )(*operands)


def main(core, first, other):
    half = bf16(CHIPS, PAIR, HEAD_SIZE)
    return call(
        main_kernel, (half, half, half),
        [SMEM, VMEM, VMEM], (VMEM, VMEM, VMEM),
        [pltpu.SMEM((CHIPS,), jnp.int32)] * 2
        + [pltpu.VMEM((CHIPS, PAIR), jnp.int32)]
        + [pltpu.VMEM((REACH + CHIPS + 1, ROWS, HEAD_SIZE), jnp.float32)] * 4
        + [pltpu.VMEM((WIDEST * ROWS, PAIR), jnp.float32)] * (3 * AT_ONCE),
        (core, first, other),
        flops=1 << 32,
    )


def body(queries, keys, values, dout, segments):
    swap = [(i, i ^ 1) for i in range(CHIPS * CORES)]
    planes = [[CORES * n + c for n in range(CHIPS)] for c in range(CORES)]
    core = (lax.axis_index("blk") % CORES).astype(jnp.int32).reshape(1)
    packed = call(
        pack_kernel, bf16(CHIPS, IN_ROWS, HEAD_SIZE), [HBM] * 5, VMEM,
        [
            pltpu.VMEM((ROWS, 2 * CHIPS * HEAD_SIZE), jnp.bfloat16),
            pltpu.VMEM((ROWS, CHIPS * HEAD_SIZE), jnp.bfloat16),
            pltpu.VMEM((ROWS, CHIPS * HEAD_SIZE), jnp.bfloat16),
            pltpu.VMEM((ROWS, 2 * CHIPS * HEAD_SIZE), jnp.bfloat16),
            pltpu.VMEM((1, ROWS), jnp.int32),
            pltpu.SemaphoreType.DMA((5,)),
        ],
        [
            pltpu.with_memory_space_constraint(a, pltpu.HBM)
            for a in (queries, keys, values, dout, segments.reshape(1, ROWS))
        ],
    )
    first = lax.all_to_all(packed, "blk", 0, 0, tiled=True, axis_index_groups=planes)
    other = lax.ppermute(first[:, KV_AT:, :], "blk", swap)
    dq, keep, send = main(core, first, other)
    got = lax.ppermute(send, "blk", swap)
    joined = call(
        join_kernel, bf16(CHIPS, 2 * PAIR, HEAD_SIZE), [VMEM] * 3, VMEM, [], (dq, keep, got)
    )
    back = lax.all_to_all(joined, "blk", 0, 0, tiled=True, axis_index_groups=planes)
    narrow = bf16(ROWS, CHIPS * HEAD_SIZE)
    return call(
        unpack_kernel, (bf16(ROWS, 2 * CHIPS * HEAD_SIZE), narrow, narrow), [VMEM], (HBM,) * 3,
        [
            pltpu.VMEM((ROWS, 2 * CHIPS * HEAD_SIZE), jnp.bfloat16),
            pltpu.VMEM((ROWS, CHIPS * HEAD_SIZE), jnp.bfloat16),
            pltpu.VMEM((ROWS, CHIPS * HEAD_SIZE), jnp.bfloat16),
            pltpu.SemaphoreType.DMA((3,)),
        ],
        (back,),
    )


def solution(mesh):
    rows = P(("grp", "blk"), None)
    in_specs = (rows, rows, rows, rows, P(("grp", "blk")))
    return jax.shard_map(body, mesh=mesh, in_specs=in_specs, out_specs=(rows, rows, rows), check_vma=False)
```

```python
import functools
import math
import jax
import jax.numpy as jnp
from jax import lax
from jax.experimental import pallas as pl
from jax.experimental.pallas import tpu as pltpu
from jax.sharding import PartitionSpec as P

HEAD_SIZE = 128
DOCS = 8
CHIPS = 8
CORES = 2
ROWS = 128
PAIR = CORES * ROWS
SEG_ROWS = 16
DO_AT = PAIR
KV_AT = 2 * PAIR
KV_ROWS = 2 * ROWS + SEG_ROWS
IN_ROWS = KV_AT + KV_ROWS
TOKENS = CHIPS * PAIR
WIDEST = 9
REACH = 4
LESS = 2
AT_ONCE = 2

score_scale = 1.0 / 12.0
cap_value = 50.0
to_cap = score_scale / cap_value
cap_log2 = cap_value * math.log2(math.e)

NT = (((1,), (1,)), ((), ()))
TN = (((0,), (0,)), ((), ()))
VMEM_LIMIT = 32 * 1024 * 1024

ANY = pl.BlockSpec(memory_space=pl.ANY)
HBM = pl.BlockSpec(memory_space=pltpu.HBM)
VMEM = pl.BlockSpec(memory_space=pltpu.VMEM)
SMEM = pl.BlockSpec(memory_space=pltpu.SMEM)


def bf16(*shape):
    return jax.ShapeDtypeStruct(shape, jnp.bfloat16)


def columns(h):
    return pl.ds(h * HEAD_SIZE, HEAD_SIZE)


def pack_kernel(q_ref, k_ref, v_ref, do_ref, seg_ref, out_ref, q_s, k_s, v_s, do_s, seg_s, sem):
    held = (q_s, do_s, k_s, v_s, seg_s)
    copies = [
        pltpu.make_async_copy(a, b, sem.at[n])
        for n, (a, b) in enumerate(zip((q_ref, do_ref, k_ref, v_ref, seg_ref), held))
    ]
    for copy in copies:
        copy.start()
    for copy, ref, at in zip(copies, held, (0, DO_AT)):
        copy.wait()
        for m in range(CHIPS):
            for part in range(2):
                out_ref[m, at + part * ROWS : at + (part + 1) * ROWS, :] = ref[:, columns(2 * m + part)]
    for copy, ref, at in zip(copies[2:], held[2:], (KV_AT, KV_AT + ROWS)):
        copy.wait()
        for m in range(CHIPS):
            out_ref[m, at : at + ROWS, :] = ref[:, columns(m)]
    copies[-1].wait()
    seg = jnp.broadcast_to(seg_s[...].astype(jnp.float32), (SEG_ROWS, ROWS))
    for m in range(CHIPS):
        out_ref[m, KV_AT + 2 * ROWS :, :] = seg.astype(jnp.bfloat16)


def unpack_kernel(in_ref, dq_ref, dk_ref, dv_ref, dq_s, dk_s, dv_s, sem):
    started = []

    def send(held, out):
        started.append(pltpu.make_async_copy(held, out, sem.at[len(started)]))
        started[-1].start()

    for m in range(CHIPS):
        for part in range(2):
            dq_s[:, columns(2 * m + part)] = in_ref[m, part * ROWS : (part + 1) * ROWS, :]
        if m % 4 == 3:
            wide = pl.ds((m - 3) * PAIR, 4 * PAIR)
            send(dq_s.at[:, wide], dq_ref.at[:, wide])
    for held, out, at in ((dk_s, dk_ref, PAIR), (dv_s, dv_ref, PAIR + ROWS)):
        for m in range(CHIPS):
            held[:, columns(m)] = in_ref[m, at : at + ROWS, :]
        send(held, out)
    for copy in started:
        copy.wait()


def seen_blocks(n, core, width, in_ref, other_ref):
    for i in range(width):
        if i % 2 == 0:
            chip, ref, at = jnp.maximum(n - i // 2, 0), in_ref, KV_AT
        else:
            chip, ref, at = jnp.maximum(n - (i + 1) // 2 + core, 0), other_ref, 0
        yield i, 2 * n + core - i, chip, ref.at[chip, pl.ds(at, ROWS)], ref.at[chip, pl.ds(at + ROWS, ROWS)]


def by_width(width, case):
    def choose(least, most):
        if least == most:
            case(least)
            return
        middle = (least + most) // 2

        @pl.when(width <= middle)
        def _():
            choose(least, middle)

        @pl.when(width > middle)
        def _():
            choose(middle + 1, most)

    choose(1, WIDEST)


def main_kernel(
    core_ref, in_ref, other_ref, dq_ref, keep_ref, send_ref, order_ref, width_ref, first_s, *work
):
    core = core_ref[0]
    dk_s, dv_s, work = work[0:2], work[2:4], work[4:]
    for sum_s in (*dk_s, *dv_s):
        sum_s[REACH : REACH + CHIPS] = jnp.zeros((CHIPS, ROWS, HEAD_SIZE), jnp.float32)

    mine = jnp.concatenate(
        [in_ref[n, KV_AT + 2 * ROWS :, :][:1].astype(jnp.float32) for n in range(CHIPS)], axis=0
    )
    theirs = jnp.concatenate([other_ref[n, 2 * ROWS :, :][:1].astype(jnp.float32) for n in range(CHIPS)], axis=0)
    first = jnp.zeros_like(mine)
    for d in range(1, DOCS):
        below = jnp.where(mine < float(d), 1.0, 0.0) + jnp.where(theirs < float(d), 1.0, 0.0)
        start = jnp.sum(jnp.sum(below, axis=1, keepdims=True), axis=0, keepdims=True)
        first = jnp.where(mine == float(d), start, first)
    first = first.astype(jnp.int32)
    first_s[:, 0:ROWS] = first
    first_s[:, ROWS:] = first

    widths = [2 * n + core + 1 - jnp.min(first[n : n + 1, :]) // ROWS for n in range(CHIPS)]
    for n in range(CHIPS):
        before = [widths[m] <= widths[n] if m < n else widths[m] < widths[n] for m in range(CHIPS) if m != n]
        rank = sum(x.astype(jnp.int32) for x in before)
        order_ref[rank] = n
        width_ref[rank] = widths[n]

    def tiles_at_once(first_at, less, width):
        widths = (width - less, width)
        tiles = [order_ref[first_at + u] for u in range(AT_ONCE)]
        q = [in_ref[n, 0:PAIR, :] for n in tiles]
        do = [in_ref[n, DO_AT : DO_AT + PAIR, :] for n in tiles]
        start = [first_s[pl.ds(n, 1), :] for n in tiles]
        seen = [list(seen_blocks(n, core, w, in_ref, other_ref)) for n, w in zip(tiles, widths)]
        key_at = lax.broadcasted_iota(jnp.int32, (ROWS, PAIR), 0)
        query_at = lax.broadcasted_iota(jnp.int32, (ROWS, PAIR), 1) % ROWS
        total = [jnp.zeros((8, PAIR), jnp.float32) for _ in tiles]
        delta = [jnp.zeros((8, PAIR), jnp.float32) for _ in tiles]
        for j in range(width):
            at = pl.ds(j * ROWS, ROWS)
            for u in range(AT_ONCE):
                if j >= widths[u]:
                    continue
                e_s, g_s, dp_s = work[3 * u : 3 * u + 3]
                _, block, _, k, v = seen[u][j]
                raw = lax.dot_general(k[...], q[u], NT, preferred_element_type=jnp.float32)
                dprob = lax.dot_general(v[...], do[u], NT, preferred_element_type=jnp.float32)
                capped = jnp.tanh(raw * to_cap)
                expo = jnp.exp2(capped * cap_log2)
                visible = key_at >= start[u] - block * ROWS
                if j == 0:
                    visible = visible & (key_at <= query_at)
                expo = jnp.where(visible, expo, 0.0)
                total[u] += jnp.sum(expo.reshape(ROWS // 8, 8, PAIR), axis=0)
                delta[u] += jnp.sum((expo * dprob).reshape(ROWS // 8, 8, PAIR), axis=0)
                e_s[at, :] = expo
                g_s[at, :] = 1.0 - capped * capped
                dp_s[at, :] = dprob
        dscores = [[] for _ in tiles]
        inverse = [1.0 / jnp.sum(x, axis=0, keepdims=True) for x in total]
        delta = [jnp.sum(x, axis=0, keepdims=True) * y for x, y in zip(delta, inverse)]
        for u in range(AT_ONCE):
            e_s, g_s, dp_s = work[3 * u : 3 * u + 3]
            for j in range(widths[u]):
                at = pl.ds(j * ROWS, ROWS)
                prob = e_s[at, :] * inverse[u]
                low = prob.astype(jnp.bfloat16)
                dscore = (prob * (dp_s[at, :] - delta[u]) * g_s[at, :]).astype(jnp.bfloat16)
                which = j % 2
                place = pl.ds(tiles[u] + (core if which else 0), REACH + 1)
                place = REACH - (j + 1) // 2, place
                dv_s[which].at[place[1]][place[0]] += jnp.dot(low, do[u], preferred_element_type=jnp.float32)
                dk_s[which].at[place[1]][place[0]] += jnp.dot(dscore, q[u], preferred_element_type=jnp.float32)
                dscores[u].append(dscore)
        for u in range(AT_ONCE):
            keys = jnp.concatenate([x[3][...] for x in seen[u]], axis=0)
            dscore = jnp.concatenate(dscores[u], axis=0)
            dq = lax.dot_general(dscore, keys, TN, preferred_element_type=jnp.float32)
            dq_ref[tiles[u]] = (dq * score_scale).astype(jnp.bfloat16)

    @pl.loop(0, CHIPS // AT_ONCE)
    def _(group):
        first_at = group * AT_ONCE
        widest = width_ref[first_at + 1]
        gap = widest - width_ref[first_at]

        def pair(width):
            if width <= LESS:
                tiles_at_once(first_at, 0, width)
                return

            @pl.when(gap < LESS)
            def _():
                tiles_at_once(first_at, 0, width)

            @pl.when(gap >= LESS)
            def _():
                tiles_at_once(first_at, LESS, width)

        by_width(widest, pair)

    for ref, dk, dv in zip((keep_ref, send_ref), dk_s, dv_s):
        ref[:, 0:ROWS, :] = (dk[REACH : REACH + CHIPS] * score_scale).astype(jnp.bfloat16)
        ref[:, ROWS:, :] = dv[REACH : REACH + CHIPS].astype(jnp.bfloat16)


def join_kernel(dq_ref, keep_ref, got_ref, out_ref):
    out_ref[:, 0:PAIR, :] = dq_ref[...]
    total = keep_ref[...].astype(jnp.float32) + got_ref[...].astype(jnp.float32)
    out_ref[:, PAIR:, :] = total.astype(jnp.bfloat16)


def call(kernel, out_shape, in_specs, out_specs, scratch, operands, flops=0):
    return pl.pallas_call(
        kernel,
        out_shape=out_shape,
        in_specs=in_specs,
        out_specs=out_specs,
        scratch_shapes=scratch,
        cost_estimate=pl.CostEstimate(flops=flops, bytes_accessed=1 << 20, transcendentals=0),
        compiler_params=pltpu.CompilerParams(vmem_limit_bytes=VMEM_LIMIT),
    )(*operands)


def main(core, first, other):
    half = bf16(CHIPS, PAIR, HEAD_SIZE)
    return call(
        main_kernel, (half, half, half),
        [SMEM, VMEM, VMEM], (VMEM, VMEM, VMEM),
        [pltpu.SMEM((CHIPS,), jnp.int32)] * 2
        + [pltpu.VMEM((CHIPS, PAIR), jnp.int32)]
        + [pltpu.VMEM((REACH + CHIPS + 1, ROWS, HEAD_SIZE), jnp.float32)] * 4
        + [pltpu.VMEM((WIDEST * ROWS, PAIR), jnp.float32)] * (3 * AT_ONCE),
        (core, first, other),
        flops=1 << 32,
    )


def body(queries, keys, values, dout, segments):
    swap = [(i, i ^ 1) for i in range(CHIPS * CORES)]
    planes = [[CORES * n + c for n in range(CHIPS)] for c in range(CORES)]
    core = (lax.axis_index("blk") % CORES).astype(jnp.int32).reshape(1)
    packed = call(
        pack_kernel, bf16(CHIPS, IN_ROWS, HEAD_SIZE), [HBM] * 5, VMEM,
        [
            pltpu.VMEM((ROWS, 2 * CHIPS * HEAD_SIZE), jnp.bfloat16),
            pltpu.VMEM((ROWS, CHIPS * HEAD_SIZE), jnp.bfloat16),
            pltpu.VMEM((ROWS, CHIPS * HEAD_SIZE), jnp.bfloat16),
            pltpu.VMEM((ROWS, 2 * CHIPS * HEAD_SIZE), jnp.bfloat16),
            pltpu.VMEM((1, ROWS), jnp.int32),
            pltpu.SemaphoreType.DMA((5,)),
        ],
        [
            pltpu.with_memory_space_constraint(a, pltpu.HBM)
            for a in (queries, keys, values, dout, segments.reshape(1, ROWS))
        ],
    )
    first = lax.all_to_all(packed, "blk", 0, 0, tiled=True, axis_index_groups=planes)
    other = lax.ppermute(first[:, KV_AT:, :], "blk", swap)
    dq, keep, send = main(core, first, other)
    got = lax.ppermute(send, "blk", swap)
    joined = call(
        join_kernel, bf16(CHIPS, 2 * PAIR, HEAD_SIZE), [VMEM] * 3, VMEM, [], (dq, keep, got)
    )
    back = lax.all_to_all(joined, "blk", 0, 0, tiled=True, axis_index_groups=planes)
    narrow = bf16(ROWS, CHIPS * HEAD_SIZE)
    return call(
        unpack_kernel, (bf16(ROWS, 2 * CHIPS * HEAD_SIZE), narrow, narrow), [VMEM], (HBM,) * 3,
        [
            pltpu.VMEM((ROWS, 2 * CHIPS * HEAD_SIZE), jnp.bfloat16),
            pltpu.VMEM((ROWS, CHIPS * HEAD_SIZE), jnp.bfloat16),
            pltpu.VMEM((ROWS, CHIPS * HEAD_SIZE), jnp.bfloat16),
            pltpu.SemaphoreType.DMA((4,)),
        ],
        (back,),
    )


def solution(mesh):
    rows = P(("grp", "blk"), None)
    in_specs = (rows, rows, rows, rows, P(("grp", "blk")))
    return jax.shard_map(body, mesh=mesh, in_specs=in_specs, out_specs=(rows, rows, rows), check_vma=False)
```
